32 devices in a mesh: groups: 1, wide: 32 (over z, y, x, core).
Axes of the slice: x: 2, y: 2, z: 4, core: 2. Of those that a mesh axis runs over, the one named last changes fastest.
Arguments:
- trial_bands: bfloat16 [1, 2, 3, 192, 192, 192], P('groups', None, None, 'wide'), may hold values from -160 to 160, as said below
- locked_bands: bfloat16 [4, 2, 3, 192, 192, 192], P('groups', None, None, 'wide'), may hold values from -240 to 240, as said below
- inv_diag: float32 [3, 192, 192, 192], P('groups', None, 'wide'), may hold values from 0.1 to 1
- inv_corr: float32 [3, 192, 192, 192], P('groups', None, 'wide'), may hold values from -0.3 to 0.3
Outputs:
- applied: bfloat16 [1, 2, 3, 192, 192, 192], P('groups', None, None, 'wide')
- rayleigh: float32 [2, 1, 1], P('groups')
The draws below stay inside these ranges and needn't reach their ends.
Inputs may be any that keep to these rules, and one draw needn't show every extreme that they name: `trial_bands`: sums of locked and independent fields, bounded. `locked_bands`: the locked bands are linearly independent.
All inputs are finite; a program needn't handle non-finite values.
Results may differ from the reference program's by a relative error of at most 0.0013.
Values sent between devices are 32-bit elements; how exact they have to be, the bound alone decides.
A program may use at most 128 MiB of HBM per device.

```python
import math
import jax
import jax.numpy as jnp
from jax import lax

NG = 192
B = 1
K = 4


def signed_axis(length):
    indices = jnp.arange(length, dtype=jnp.int32)
    shifted = jnp.where(indices < length // 2, indices, indices - length)
    return shifted.astype(jnp.float32) / (length / 2.0)


def plane_fraction():
    indices = jnp.arange(NG, dtype=jnp.int32).astype(jnp.float32)
    return (indices / float(NG))[:, None, None]


def rise_profile():
    frac = plane_fraction()
    return 0.6 + 0.9 * frac


def fall_profile():
    frac = plane_fraction()
    return 2.0 - 1.6 * frac


def envelope_field():
    wave_axis = signed_axis(NG)
    radius = wave_axis[:, None, None] ** 2 + wave_axis[None, :, None] ** 2 + wave_axis[None, None, :] ** 2
    return 1.5 / (1.0 + radius)


def rough_field(key, length):
    return jnp.clip(jax.random.normal(key, (length, 2, 3, NG, NG, NG), jnp.float32), -6.0, 6.0)


def locked_base(key):
    noise_field = rough_field(jax.random.fold_in(key, 101), K)
    offdiag = jax.random.uniform(jax.random.fold_in(key, 102), (K, K), jnp.float32, -1.0, 1.0) * (0.75 / max(K - 1, 1))
    identity = jnp.eye(K, dtype=jnp.float32)
    mixing = identity + offdiag * (1.0 - identity)
    mixed = jnp.einsum('kj,jpcxyz->kpcxyz', mixing, noise_field, precision=lax.Precision.HIGHEST)
    return mixed * (envelope_field() * rise_profile())


def draw_locked_bands(key, part):
    base_field = locked_base(key)
    scales = jnp.exp(jax.random.uniform(jax.random.fold_in(key, 103), (K,), jnp.float32, 0.0, math.log(10.0)))
    return (base_field * scales[:, None, None, None, None, None]).astype(jnp.bfloat16)


def draw_trial_bands(key, part):
    base_field = locked_base(key)
    coeffs = jax.random.uniform(jax.random.fold_in(key, 104), (B, K), jnp.float32, -0.6, 0.6)
    own_part = rough_field(jax.random.fold_in(key, 105), B) * (envelope_field() * rise_profile())
    mixed = jnp.einsum('bk,kpcxyz->bpcxyz', coeffs, base_field, precision=lax.Precision.HIGHEST)
    return (mixed * fall_profile() + own_part).astype(jnp.bfloat16)


def block_levels(own_key, extent, split, smallest, high):
    factor_of, own = 1.0, jax.random.fold_in(own_key, 6)
    for axis_at, shards_of in split:
        draws = jnp.exp(jax.random.uniform(jax.random.fold_in(own, axis_at), (shards_of,), jnp.float32, smallest / len(split), high / len(split)))
        factor_of = factor_of * jnp.repeat(draws, extent[axis_at] // shards_of).reshape([-1 if axis == axis_at else 1 for axis in range(len(extent))])
    return factor_of


def setup_inputs(seed: int = 0, part: int = 0) -> dict:
    streams_of = jax.random.split(jax.random.key(seed), 5)
    part_splits = jax.random.split(jax.random.fold_in(streams_of[4], part), 5)
    return {
        "trial_bands": draw_trial_bands(jax.random.fold_in(jax.random.fold_in(streams_of[4], part), 71), part),
        "locked_bands": draw_locked_bands(jax.random.fold_in(jax.random.fold_in(streams_of[4], part), 71), part),
        "inv_diag": jnp.clip(jnp.exp(math.log(1.0) - 2.3025851 * jax.random.uniform(part_splits[2], (3, NG, NG, NG), jnp.float32) ** block_levels(part_splits[2], (3, NG, NG, NG), ((2, 32),), -0.2, 0.2)), 0.1, 1.0),
        "inv_corr": jnp.clip(jax.random.uniform(part_splits[3], (3, NG, NG, NG), jnp.float32, -0.3, 0.3) * block_levels(part_splits[3], (3, NG, NG, NG), ((2, 32),), -0.4, 0.0), -0.3, 0.3),
    }


highest = lax.Precision.HIGHEST

def signed_wave(length):
    indices = jnp.arange(length, dtype=jnp.int32)
    shifted = jnp.where(indices < length // 2, indices, indices - length)
    return shifted.astype(jnp.float32) / (length / 2.0)

def cross_wave(wave_x, wave_y, wave_z, vectors):
    comp_x = vectors[..., 0, :, :, :]
    comp_y = vectors[..., 1, :, :, :]
    comp_z = vectors[..., 2, :, :, :]
    along_x = wave_x[:, None, None]
    along_y = wave_y[None, :, None]
    along_z = wave_z[None, None, :]
    return jnp.stack([along_y * comp_z - along_z * comp_y, along_z * comp_x - along_x * comp_z, along_x * comp_y - along_y * comp_x], axis=-4)

def apply_tensor(vectors, inv_diag, inv_corr):
    coupling_xy = inv_corr[0] * jnp.sqrt(inv_diag[0] * inv_diag[1])
    coupling_xz = inv_corr[1] * jnp.sqrt(inv_diag[0] * inv_diag[2])
    coupling_yz = inv_corr[2] * jnp.sqrt(inv_diag[1] * inv_diag[2])
    comp_x = vectors[..., 0, :, :, :]
    comp_y = vectors[..., 1, :, :, :]
    comp_z = vectors[..., 2, :, :, :]
    out_x = inv_diag[0] * comp_x + coupling_xy * comp_y + coupling_xz * comp_z
    out_y = coupling_xy * comp_x + inv_diag[1] * comp_y + coupling_yz * comp_z
    out_z = coupling_xz * comp_x + coupling_yz * comp_y + inv_diag[2] * comp_z
    return jnp.stack([out_x, out_y, out_z], axis=-4)

def inner_sum(left_rows, right_rows):
    return jnp.einsum('an,bn->ab', left_rows.astype(jnp.float32), right_rows.astype(jnp.float32), preferred_element_type=jnp.float32)

def remove_locked(gram_sums, trial_re, trial_im, locked_re, locked_im):
    gram_a, gram_q, proj_re, proj_im = gram_sums
    kept_count = gram_a.shape[0]
    gram = jnp.concatenate([jnp.concatenate([gram_a, gram_q], axis=1), jnp.concatenate([gram_q.T, gram_a], axis=1)], axis=0)
    rhs_both = jnp.concatenate([proj_re, proj_im], axis=0)
    lower = jnp.linalg.cholesky(gram)
    middle = lax.linalg.triangular_solve(lower, rhs_both, left_side=True, lower=True)
    coef = lax.linalg.triangular_solve(lower, middle, left_side=True, lower=True, transpose_a=True)
    coef_one = coef[:kept_count]
    coef_two = coef[kept_count:]
    locked_re32 = locked_re.astype(jnp.float32)
    locked_im32 = locked_im.astype(jnp.float32)
    out_re = trial_re.astype(jnp.float32) - jnp.einsum('ab,an->bn', coef_one, locked_re32, precision=highest) + jnp.einsum('ab,an->bn', coef_two, locked_im32, precision=highest)
    out_im = trial_im.astype(jnp.float32) - jnp.einsum('ab,an->bn', coef_one, locked_im32, precision=highest) - jnp.einsum('ab,an->bn', coef_two, locked_re32, precision=highest)
    return (out_re, out_im)

def reference(trial_bands, locked_bands, inv_diag, inv_corr):
    band_count = trial_bands.shape[0]
    kept_count = locked_bands.shape[0]
    trial_re = trial_bands[:, 0].reshape(band_count, -1)
    trial_im = trial_bands[:, 1].reshape(band_count, -1)
    locked_re = locked_bands[:, 0].reshape(kept_count, -1)
    locked_im = locked_bands[:, 1].reshape(kept_count, -1)
    gram_a = inner_sum(locked_re, locked_re) + inner_sum(locked_im, locked_im)
    gram_q = inner_sum(locked_im, locked_re) - inner_sum(locked_re, locked_im)
    proj_re = inner_sum(locked_re, trial_re) + inner_sum(locked_im, trial_im)
    proj_im = inner_sum(locked_re, trial_im) - inner_sum(locked_im, trial_re)
    flat_re, flat_im = remove_locked((gram_a, gram_q, proj_re, proj_im), trial_re, trial_im, locked_re, locked_im)
    shape_one = (band_count, 3, NG, NG, NG)
    wave_axis = signed_wave(NG)

    def apply_band(inputs):
        part_re, part_im = inputs
        curled_re = -cross_wave(wave_axis, wave_axis, wave_axis, part_im)
        curled_im = cross_wave(wave_axis, wave_axis, wave_axis, part_re)
        spatial = jnp.fft.ifftn(lax.complex(curled_re, curled_im), axes=(1, 2, 3), norm='ortho')
        weighted_re = apply_tensor(jnp.real(spatial), inv_diag, inv_corr)
        weighted_im = apply_tensor(jnp.imag(spatial), inv_diag, inv_corr)
        spectral = jnp.fft.fftn(lax.complex(weighted_re, weighted_im), axes=(1, 2, 3), norm='ortho')
        spec_re = jnp.real(spectral)
        spec_im = jnp.imag(spectral)
        return (-cross_wave(wave_axis, wave_axis, wave_axis, spec_im), cross_wave(wave_axis, wave_axis, wave_axis, spec_re))
    applied_re, applied_im = lax.map(apply_band, (flat_re.reshape(shape_one), flat_im.reshape(shape_one)))
    applied = jnp.stack([applied_re, applied_im], axis=1).astype(jnp.bfloat16)
    rows_re = applied_re.reshape(band_count, -1)
    rows_im = applied_im.reshape(band_count, -1)
    scale_all = 1.0 / float(NG * NG * NG)
    rayleigh_re = (jnp.einsum('an,bn->ab', flat_re, rows_re, precision=highest) + jnp.einsum('an,bn->ab', flat_im, rows_im, precision=highest)) * scale_all
    rayleigh_im = (jnp.einsum('an,bn->ab', flat_re, rows_im, precision=highest) - jnp.einsum('an,bn->ab', flat_im, rows_re, precision=highest)) * scale_all
    return (applied, jnp.stack([rayleigh_re, rayleigh_im], axis=0))
```

```python
import functools
import math

import jax
import jax.numpy as jnp
import numpy as np
from jax import lax
from jax.experimental import pallas as pl
from jax.experimental.pallas import tpu as pltpu
from jax.sharding import PartitionSpec as P

HI = lax.Precision.HIGHEST
F32 = jnp.float32
BF16 = jnp.bfloat16
VMEM_LIMIT = 56 * 1024 * 1024


def signed(length):
    g = np.arange(length)
    return np.where(g < length // 2, g, g - length).astype(np.float32) / np.float32(length / 2.0)


def cos_sin(length, orient):
    g = np.arange(length)
    ang = (g[:, None] * g[None, :] % length) * (2.0 * math.pi / length)
    return np.cos(ang) / math.sqrt(length), orient * np.sin(ang) / math.sqrt(length)


def split_np(table):
    table = table.astype(np.float32)
    high = table.astype(BF16)
    low = (table - high.astype(np.float32)).astype(BF16)
    return np.stack([high, low])


def lane_order(length):
    cut = 2 * length // 3
    part = np.concatenate([np.zeros(length), np.ones(length)]).astype(int)
    pos = np.concatenate([np.arange(length), np.arange(cut, length), np.arange(cut)])
    return part, pos


def right_table(length, orient):
    cos, sin = cos_sin(length, orient)
    full = np.block([[cos, sin], [-sin, cos]])
    part, pos = lane_order(length)
    return full[:, part * length + pos]


def right_table_back(length, orient):
    cos, sin = cos_sin(length, orient)
    full = np.block([[cos, sin], [-sin, cos]])
    part, pos = lane_order(length)
    return full[part * length + pos, :]


def left_table(length, orient, perm_rows=None, perm_cols=None):
    cos, sin = cos_sin(length, orient)
    if perm_rows is not None:
        cos, sin = cos[perm_rows], sin[perm_rows]
    if perm_cols is not None:
        cos, sin = cos[:, perm_cols], sin[:, perm_cols]
    return np.concatenate([cos, sin], axis=1)


def split(x):
    high = x.astype(BF16)
    low = (x - high.astype(F32)).astype(BF16)
    return high, low


def dot(a, b):
    return jnp.dot(a, b, preferred_element_type=F32)


def dot3(a, b):
    return dot(a[0], b[0]) + (dot(a[0], b[1]) + dot(a[1], b[0]))


def times_i(tiles):
    t0, t1, t2 = tiles
    half = t1.shape[1] // 2
    lane = lax.broadcasted_iota(jnp.int32, t1.shape, 1)
    mid = pltpu.roll(t1, half, 1)
    mid = jnp.where(lane < half, -mid, mid)
    return [-t2, mid, t0]


def left_dft(table, tiles, turned):
    rows = jnp.concatenate(
        [jnp.concatenate(tiles, axis=1), jnp.concatenate(turned, axis=1)], axis=0
    )
    return dot3(table, split(rows))


def gram_kernel(kept, locked_ref, trial_ref, out_ref, acc_ref):
    step = pl.program_id(0)
    grid_len = locked_ref.shape[4]
    fields = 2 * kept + 2

    @pl.when(step == 0)
    def _():
        acc_ref[...] = jnp.zeros_like(acc_ref)

    total = None
    for comp in range(3):
        for at in range(0, grid_len, 16):
            parts = [locked_ref[k, p, comp, 0, at:at + 16, :] for p in range(2) for k in range(kept)]
            parts += [trial_ref[0, p, comp, 0, at:at + 16, :] for p in range(2)]
            rows = jnp.concatenate(parts, axis=0)
            one = lax.dot_general(
                rows, rows, (((1,), (1,)), ((), ())), preferred_element_type=F32
            )
            total = one if total is None else total + one
    acc_ref[...] += total

    @pl.when(step == pl.num_programs(0) - 1)
    def _():
        acc = acc_ref[...]
        size = fields * 16
        row = lax.broadcasted_iota(jnp.int32, (size, size), 0)
        col = lax.broadcasted_iota(jnp.int32, (size, size), 1)
        kept_only = jnp.where((row & 15) == (col & 15), acc, 0.0)
        by_row = jnp.sum(kept_only.reshape(fields, 16, size), axis=1)
        pick_r = lax.broadcasted_iota(jnp.int32, (size, 128), 0)
        pick_c = lax.broadcasted_iota(jnp.int32, (size, 128), 1)
        pick = jnp.where((pick_r >> 4) == pick_c, 1.0, 0.0)
        small = jnp.dot(by_row, pick, precision=HI, preferred_element_type=F32)
        out_ref[...] = jnp.concatenate([small, jnp.zeros((16 - fields, 128), F32)], axis=0)


def peer_of(me, k, n):
    if n & (n - 1) == 0:
        return lax.bitwise_xor(me, k)
    return lax.rem(me + k, n)


def greet(me, n):
    barrier = pltpu.get_barrier_semaphore()

    def hello(k, carry):
        pl.semaphore_signal(
            barrier,
            inc=1,
            device_id={"wide": lax.rem(me + k, n)},
            device_id_type=pl.DeviceIdType.MESH,
        )
        return carry

    lax.fori_loop(1, n, hello, 0)
    pl.semaphore_wait(barrier, n - 1)


def sum_kernel(n, x_ref, o_ref, buf_ref, send, recv):
    me = lax.axis_index("wide")
    buf_ref[0] = x_ref[...]
    greet(me, n)

    def make(k):
        peer = lax.rem(me + k, n)
        return pltpu.make_async_remote_copy(
            src_ref=x_ref,
            dst_ref=buf_ref.at[k],
            send_sem=send.at[k],
            recv_sem=recv.at[k],
            device_id={"wide": peer},
            device_id_type=pl.DeviceIdType.MESH,
        )

    def go(k, carry):
        make(k).start()
        return carry

    def finish(k, carry):
        make(k).wait()
        return carry

    lax.fori_loop(1, n, go, 0)
    lax.fori_loop(1, n, finish, 0)
    o_ref[...] = jnp.sum(buf_ref[...], axis=0)


def sum_small(x, n):
    return pl.pallas_call(
        functools.partial(sum_kernel, n),
        out_shape=jax.ShapeDtypeStruct(x.shape, x.dtype),
        in_specs=[pl.BlockSpec(memory_space=pltpu.VMEM)],
        out_specs=pl.BlockSpec(memory_space=pltpu.VMEM),
        scratch_shapes=[
            pltpu.VMEM((n,) + x.shape, x.dtype),
            pltpu.SemaphoreType.DMA((n,)),
            pltpu.SemaphoreType.DMA((n,)),
        ],
        compiler_params=pltpu.CompilerParams(collective_id=0, has_side_effects=True),
    )(x)


def out_kernel(sizes, coef_ref, wave_ref, locked_ref, trial_ref, qy_ref, qz_ref, tz_ref, ty_ref, out_ref):
    n, rows, lx, ly, kept, grid_len = sizes
    step = pl.program_id(0)
    qx = wave_ref[step]
    qy = qy_ref[...]
    qz = qz_ref[...]
    one = [coef_ref[k] for k in range(kept)]
    two = [coef_ref[kept + k] for k in range(kept)]
    real, imag = [], []
    for comp in range(3):
        re = trial_ref[0, 0, comp, 0].astype(F32)
        im = trial_ref[0, 1, comp, 0].astype(F32)
        for k in range(kept):
            lre = locked_ref[k, 0, comp, 0].astype(F32)
            lim = locked_ref[k, 1, comp, 0].astype(F32)
            re = re - one[k] * lre + two[k] * lim
            im = im - one[k] * lim - two[k] * lre
        real.append(re)
        imag.append(im)

    def cross(v):
        return [qy * v[2] - qz * v[1], qz * v[0] - qx * v[2], qx * v[1] - qy * v[0]]

    curl_re = [-v for v in cross(imag)]
    curl_im = cross(real)
    for comp in range(3):
        out = dot3(split(curl_re[comp]), (tz_ref[0, :grid_len], tz_ref[1, :grid_len]))
        out += dot3(split(curl_im[comp]), (tz_ref[0, grid_len:], tz_ref[1, grid_len:]))
        tiles = [out[:, t * 128:(t + 1) * 128] for t in range(3)]
        out = left_dft((ty_ref[0], ty_ref[1]), tiles, times_i(tiles))
        for j in range(ly):
            for t in range(3):
                at = t * rows + step * (3 * ly) + comp * ly + j
                out_ref[pl.ds(at, n, stride=3 * rows), :] = out[j * n:(j + 1) * n, t * 128:(t + 1) * 128]


def mid_kernel(sizes, x_ref, diag_ref, corr_ref, ti_ref, tf_ref, out_ref, acc_ref):
    n, rows, lx, ly, kept, grid_len = sizes
    step = pl.program_id(0)

    @pl.when(step == 0)
    def _():
        acc_ref[...] = jnp.zeros_like(acc_ref)

    space = []
    for comp in range(3):
        tiles = []
        for t in range(3):
            at = [t * rows + x * (3 * ly) + comp * ly + step for x in range(lx)]
            tiles.append(
                jnp.concatenate([x_ref[pl.ds(a, n, stride=3 * rows), :] for a in at], axis=0)
            )
        out = left_dft((ti_ref[0], ti_ref[1]), tiles, times_i(tiles))
        space.append([out[:, t * 128:(t + 1) * 128] for t in range(3)])

    def lanes(e):
        tail = e[:, 128:]
        return [e[:, :128], jnp.concatenate([tail, tail], axis=1)]

    dx, dy, dz = diag_ref[0, 0], diag_ref[1, 0], diag_ref[2, 0]
    exy = lanes(corr_ref[0, 0] * jnp.sqrt(dx * dy))
    exz = lanes(corr_ref[1, 0] * jnp.sqrt(dx * dz))
    eyz = lanes(corr_ref[2, 0] * jnp.sqrt(dy * dz))
    exx, eyy, ezz = lanes(dx), lanes(dy), lanes(dz)
    matrix = [[exx, exy, exz], [exy, eyy, eyz], [exz, eyz, ezz]]
    sum_re = jnp.zeros((grid_len, 128), F32)
    sum_im = jnp.zeros((grid_len, 128), F32)
    for comp in range(3):
        tiles = []
        for t in range(3):
            e = [matrix[comp][b][t % 2] for b in range(3)]
            tiles.append(e[0] * space[0][t] + e[1] * space[1][t] + e[2] * space[2][t])
        turned = times_i(tiles)
        for t in range(3):
            sum_re += space[comp][t] * tiles[t]
            sum_im -= space[comp][t] * turned[t]
        out = left_dft((tf_ref[0], tf_ref[1]), tiles, turned)
        for x in range(lx):
            for t in range(3):
                at = t * rows + x * (3 * ly) + comp * ly + step
                out_ref[pl.ds(at, n, stride=3 * rows), :] = out[x * n:(x + 1) * n, t * 128:(t + 1) * 128]
    acc_ref[0:1] += jnp.sum(sum_re, axis=0, keepdims=True)
    acc_ref[1:2] += jnp.sum(sum_im, axis=0, keepdims=True)

    @pl.when(step == pl.num_programs(0) - 1)
    def _():
        for t in range(3):
            for r in range(3 * lx * ly, rows):
                value = jnp.broadcast_to(acc_ref[min(t, 1):min(t, 1) + 1], (n, 128))
                out_ref[pl.ds(t * rows + r, n, stride=3 * rows), :] = value


def home_kernel(sizes, wave_ref, x_ref, qy_ref, qz_ref, ty_ref, tz_ref, out_ref, ray_ref):
    n, rows, lx, ly, kept, grid_len = sizes
    step = pl.program_id(0)
    qx = wave_ref[step]
    qy = qy_ref[...]
    qz = qz_ref[...]
    real, imag = [], []
    for comp in range(3):
        tiles = []
        for t in range(3):
            at = [t * rows + step * (3 * ly) + comp * ly + j for j in range(ly)]
            tiles.append(
                jnp.concatenate([x_ref[pl.ds(a, n, stride=3 * rows), :] for a in at], axis=0)
            )
        out = split(left_dft((ty_ref[0], ty_ref[1]), tiles, times_i(tiles)))
        real.append(dot3(out, (tz_ref[0], tz_ref[1])))
        imag.append(dot3(out, (tz_ref[2], tz_ref[3])))

    def cross(v):
        return [qy * v[2] - qz * v[1], qz * v[0] - qx * v[2], qx * v[1] - qy * v[0]]

    for comp, (a, b) in enumerate(zip(cross(imag), cross(real))):
        out_ref[0, 0, comp, 0] = (-a).astype(BF16)
        out_ref[0, 1, comp, 0] = b.astype(BF16)

    @pl.when(step == pl.num_programs(0) - 1)
    def _():
        for p in range(2):
            ray_ref[p * n:(p + 1) * n, :] = x_ref[pl.ds(p * rows + 3 * lx * ly, n, stride=3 * rows), :]


def swap_kernel(n, x_ref, o_ref, send, recv, here):
    me = lax.axis_index("wide")
    greet(me, n)

    def make(k):
        peer = peer_of(me, k, n)
        return pltpu.make_async_remote_copy(
            src_ref=x_ref.at[peer],
            dst_ref=o_ref.at[me],
            send_sem=send.at[k],
            recv_sem=recv.at[k],
            device_id={"wide": peer},
            device_id_type=pl.DeviceIdType.MESH,
        )

    def go(k, carry):
        make(k).start()
        return carry

    def finish(k, carry):
        make(k).wait()
        return carry

    lax.fori_loop(1, n, go, 0)
    own = pltpu.make_async_copy(x_ref.at[me], o_ref.at[me], here)
    own.start()
    own.wait()
    lax.fori_loop(1, n, finish, 0)


def exchange(flat, n):
    box = flat.reshape(n, flat.shape[0] // n, flat.shape[1])
    return lax.all_to_all(box, "wide", 0, 0, tiled=True).reshape(flat.shape)


def per_device(trial_bands, locked_bands, inv_diag, inv_corr):
    kept = locked_bands.shape[0]
    lx = trial_bands.shape[3]
    grid_len = trial_bands.shape[4]
    n = grid_len // lx
    ly = inv_diag.shape[2]
    rows = (3 * lx * ly + 8) // 8 * 8
    sizes = (n, rows, lx, ly, kept, grid_len)
    me = lax.axis_index("wide")
    fields = 2 * kept + 2

    def params():
        return pltpu.CompilerParams(vmem_limit_bytes=VMEM_LIMIT, dimension_semantics=("arbitrary",))

    def full(a):
        return pl.BlockSpec(a.shape, lambda i: (0,) * a.ndim)

    plane = lambda lead: pl.BlockSpec(
        (lead, 2, 3, 1, grid_len, grid_len), lambda i: (0, 0, 0, i, 0, 0)
    )
    smem = pl.BlockSpec(memory_space=pltpu.SMEM)

    part = pl.pallas_call(
        functools.partial(gram_kernel, kept),
        grid=(lx,),
        out_shape=jax.ShapeDtypeStruct((16, 128), F32),
        in_specs=[plane(kept), plane(1)],
        out_specs=pl.BlockSpec((16, 128), lambda i: (0, 0)),
        scratch_shapes=[pltpu.VMEM((fields * 16, fields * 16), F32)],
        compiler_params=params(),
    )(locked_bands, trial_bands)
    sums = sum_small(part, n)
    k2 = 2 * kept
    rr, ri = sums[:kept, :kept], sums[:kept, kept:k2]
    ir, ii = sums[kept:k2, :kept], sums[kept:k2, kept:k2]
    gram_a, gram_q = rr + ii, ir - ri
    proj_re = sums[:kept, k2:k2 + 1] + sums[kept:k2, k2 + 1:k2 + 2]
    proj_im = sums[:kept, k2 + 1:k2 + 2] - sums[kept:k2, k2:k2 + 1]
    gram = jnp.concatenate(
        [jnp.concatenate([gram_a, gram_q], axis=1), jnp.concatenate([gram_q.T, gram_a], axis=1)],
        axis=0,
    )
    rhs = jnp.concatenate([proj_re, proj_im], axis=0)
    lower = jnp.linalg.cholesky(gram)
    middle = lax.linalg.triangular_solve(lower, rhs, left_side=True, lower=True)
    coef = lax.linalg.triangular_solve(lower, middle, left_side=True, lower=True, transpose_a=True)
    coef = coef[:, 0]

    waves = signed(grid_len)
    wave_x = lax.dynamic_slice(jnp.asarray(waves), (me * lx,), (lx,))
    qy = jnp.asarray(np.broadcast_to(waves[:, None], (grid_len, grid_len)))
    qz = jnp.asarray(np.broadcast_to(waves[None, :], (grid_len, grid_len)))
    order_y = np.arange(grid_len).reshape(n, ly).T.reshape(-1)
    order_x = np.arange(grid_len).reshape(n, lx).T.reshape(-1)
    tz_out = jnp.asarray(split_np(right_table(grid_len, 1.0)))
    ty_out = jnp.asarray(split_np(left_table(grid_len, 1.0, perm_rows=order_y)))
    tx_in = jnp.asarray(split_np(left_table(grid_len, 1.0, perm_cols=order_x)))
    tx_out = jnp.asarray(split_np(left_table(grid_len, -1.0, perm_rows=order_x)))
    ty_in = jnp.asarray(split_np(left_table(grid_len, -1.0, perm_cols=order_y)))
    back = right_table_back(grid_len, -1.0)
    tz_in = jnp.asarray(
        np.concatenate([split_np(back[:, :grid_len]), split_np(back[:, grid_len:])])
    )

    flat_shape = jax.ShapeDtypeStruct((n * 3 * rows, 128), F32)
    flat_spec = pl.BlockSpec((n * 3 * rows, 128), lambda i: (0, 0))
    moved = pl.pallas_call(
        functools.partial(out_kernel, sizes),
        grid=(lx,),
        out_shape=flat_shape,
        in_specs=[smem, smem, plane(kept), plane(1), full(qy), full(qz), full(tz_out), full(ty_out)],
        out_specs=flat_spec,
        compiler_params=params(),
    )(coef, wave_x, locked_bands, trial_bands, qy, qz, tz_out, ty_out)
    moved = exchange(moved, n)

    slab = pl.BlockSpec((3, 1, grid_len, grid_len), lambda i: (0, i, 0, 0))
    weighted = pl.pallas_call(
        functools.partial(mid_kernel, sizes),
        grid=(ly,),
        out_shape=flat_shape,
        in_specs=[flat_spec, slab, slab, full(tx_in), full(tx_out)],
        out_specs=flat_spec,
        scratch_shapes=[pltpu.VMEM((8, 128), F32)],
        compiler_params=params(),
    )(moved, inv_diag.transpose(0, 2, 1, 3), inv_corr.transpose(0, 2, 1, 3), tx_in, tx_out)
    home = exchange(weighted, n)

    applied, ray = pl.pallas_call(
        functools.partial(home_kernel, sizes),
        grid=(lx,),
        out_shape=(
            jax.ShapeDtypeStruct(trial_bands.shape, BF16),
            jax.ShapeDtypeStruct((2 * n, 128), F32),
        ),
        in_specs=[smem, flat_spec, full(qy), full(qz), full(ty_in), full(tz_in)],
        out_specs=(plane(1), pl.BlockSpec((2 * n, 128), lambda i: (0, 0))),
        compiler_params=params(),
    )(wave_x, home, qy, qz, ty_in, tz_in)
    scale_all = 1.0 / float(grid_len * grid_len * grid_len)
    rayleigh = jnp.sum(ray.reshape(2, n * 128), axis=1).reshape(2, 1, 1) * scale_all
    return (applied, rayleigh)


def solution(mesh):
    in_specs = (
        P("groups", None, None, "wide", None, None),
        P("groups", None, None, "wide", None, None),
        P("groups", None, "wide", None),
        P("groups", None, "wide", None),
    )
    out_specs = (P("groups", None, None, "wide", None, None), P("groups", None, None))
    return jax.shard_map(
        per_device, mesh=mesh, in_specs=in_specs, out_specs=out_specs, check_vma=False
    )
```

```python
import functools
import math

import jax
import jax.numpy as jnp
import numpy as np
from jax import lax
from jax.experimental import pallas as pl
from jax.experimental.pallas import tpu as pltpu
from jax.sharding import PartitionSpec as P

HI = lax.Precision.HIGHEST
F32 = jnp.float32
BF16 = jnp.bfloat16
VMEM_LIMIT = 56 * 1024 * 1024


def signed(length):
    g = np.arange(length)
    return np.where(g < length // 2, g, g - length).astype(np.float32) / np.float32(length / 2.0)


def cos_sin(length, orient):
    g = np.arange(length)
    ang = (g[:, None] * g[None, :] % length) * (2.0 * math.pi / length)
    return np.cos(ang) / math.sqrt(length), orient * np.sin(ang) / math.sqrt(length)


def split_np(table):
    table = table.astype(np.float32)
    high = table.astype(BF16)
    low = (table - high.astype(np.float32)).astype(BF16)
    return np.stack([high, low])


def lane_order(length):
    cut = 2 * length // 3
    part = np.concatenate([np.zeros(length), np.ones(length)]).astype(int)
    pos = np.concatenate([np.arange(length), np.arange(cut, length), np.arange(cut)])
    return part, pos


def right_table(length, orient):
    cos, sin = cos_sin(length, orient)
    full = np.block([[cos, sin], [-sin, cos]])
    part, pos = lane_order(length)
    return full[:, part * length + pos]


def right_table_back(length, orient):
    cos, sin = cos_sin(length, orient)
    full = np.block([[cos, sin], [-sin, cos]])
    part, pos = lane_order(length)
    return full[part * length + pos, :]


def left_table(length, orient, perm_rows=None, perm_cols=None):
    cos, sin = cos_sin(length, orient)
    if perm_rows is not None:
        cos, sin = cos[perm_rows], sin[perm_rows]
    if perm_cols is not None:
        cos, sin = cos[:, perm_cols], sin[:, perm_cols]
    return np.concatenate([cos, sin], axis=0)


def split(x):
    high = x.astype(BF16)
    low = (x - high.astype(F32)).astype(BF16)
    return high, low


def dot(a, b):
    return jnp.dot(a, b, preferred_element_type=F32)


def times_i(tiles):
    t0, t1, t2 = tiles
    half = t1.shape[1] // 2
    lane = lax.broadcasted_iota(jnp.int32, t1.shape, 1)
    mid = pltpu.roll(t1, half, 1)
    mid = jnp.where(lane < half, -mid, mid)
    return [-t2, mid, t0]


def left_dft(table, tiles):
    length = table.shape[1]
    high, low = split(jnp.concatenate(tiles, axis=1))
    first = dot(table[...], high)
    both = first[:2 * length] + (first[2 * length:] + dot(table[:2 * length, :], low))
    real = [both[:length, t * 128:(t + 1) * 128] for t in range(3)]
    turned = times_i([both[length:, t * 128:(t + 1) * 128] for t in range(3)])
    return jnp.concatenate([r + i for r, i in zip(real, turned)], axis=1)


def right_dft(rows, high_table, low_table):
    count = rows.shape[0]
    high, low = split(rows)
    first = dot(jnp.concatenate([high, low], axis=0), high_table)
    return first[:count] + (first[count:] + dot(high, low_table))


def gram_kernel(kept, locked_ref, trial_ref, out_ref, acc_ref):
    step = pl.program_id(0)
    grid_len = locked_ref.shape[4]
    fields = 2 * kept + 2

    @pl.when(step == 0)
    def _():
        acc_ref[...] = jnp.zeros_like(acc_ref)

    total = None
    for comp in range(3):
        for at in range(0, grid_len, 16):
            parts = [locked_ref[k, p, comp, 0, at:at + 16, :] for p in range(2) for k in range(kept)]
            parts += [trial_ref[0, p, comp, 0, at:at + 16, :] for p in range(2)]
            rows = jnp.concatenate(parts, axis=0)
            one = lax.dot_general(
                rows, rows, (((1,), (1,)), ((), ())), preferred_element_type=F32
            )
            total = one if total is None else total + one
    acc_ref[...] += total

    @pl.when(step == pl.num_programs(0) - 1)
    def _():
        acc = acc_ref[...]
        size = fields * 16
        row = lax.broadcasted_iota(jnp.int32, (size, size), 0)
        col = lax.broadcasted_iota(jnp.int32, (size, size), 1)
        kept_only = jnp.where((row & 15) == (col & 15), acc, 0.0)
        by_row = jnp.sum(kept_only.reshape(fields, 16, size), axis=1)
        pick_r = lax.broadcasted_iota(jnp.int32, (size, 128), 0)
        pick_c = lax.broadcasted_iota(jnp.int32, (size, 128), 1)
        pick = jnp.where((pick_r >> 4) == pick_c, 1.0, 0.0)
        small = jnp.dot(by_row, pick, precision=HI, preferred_element_type=F32)
        out_ref[...] = jnp.concatenate([small, jnp.zeros((16 - fields, 128), F32)], axis=0)


def greet(me, n):
    barrier = pltpu.get_barrier_semaphore()

    def hello(k, carry):
        pl.semaphore_signal(
            barrier,
            inc=1,
            device_id={"wide": lax.rem(me + k, n)},
            device_id_type=pl.DeviceIdType.MESH,
        )
        return carry

    lax.fori_loop(1, n, hello, 0)
    pl.semaphore_wait(barrier, n - 1)


def sum_kernel(n, x_ref, o_ref, buf_ref, send, recv):
    me = lax.axis_index("wide")
    buf_ref[0] = x_ref[...]
    greet(me, n)

    def make(k):
        peer = lax.rem(me + k, n)
        return pltpu.make_async_remote_copy(
            src_ref=x_ref,
            dst_ref=buf_ref.at[k],
            send_sem=send.at[k],
            recv_sem=recv.at[k],
            device_id={"wide": peer},
            device_id_type=pl.DeviceIdType.MESH,
        )

    def go(k, carry):
        make(k).start()
        return carry

    def finish(k, carry):
        make(k).wait()
        return carry

    lax.fori_loop(1, n, go, 0)
    lax.fori_loop(1, n, finish, 0)
    o_ref[...] = jnp.sum(buf_ref[...], axis=0)


def sum_small(x, n):
    return pl.pallas_call(
        functools.partial(sum_kernel, n),
        out_shape=jax.ShapeDtypeStruct(x.shape, x.dtype),
        in_specs=[pl.BlockSpec(memory_space=pltpu.VMEM)],
        out_specs=pl.BlockSpec(memory_space=pltpu.VMEM),
        scratch_shapes=[
            pltpu.VMEM((n,) + x.shape, x.dtype),
            pltpu.SemaphoreType.DMA((n,)),
            pltpu.SemaphoreType.DMA((n,)),
        ],
        compiler_params=pltpu.CompilerParams(collective_id=0, has_side_effects=True),
    )(x)


def out_kernel(sizes, coef_ref, wave_ref, locked_ref, trial_ref, qy_ref, qz_ref, tz_ref, ty_ref, out_ref):
    n, rows, lx, ly, kept, grid_len = sizes
    step = pl.program_id(0)
    qx = wave_ref[step]
    qy = qy_ref[...]
    qz = qz_ref[...]
    one = [coef_ref[k] for k in range(kept)]
    two = [coef_ref[kept + k] for k in range(kept)]
    real, imag = [], []
    for comp in range(3):
        re = trial_ref[0, 0, comp, 0].astype(F32)
        im = trial_ref[0, 1, comp, 0].astype(F32)
        for k in range(kept):
            lre = locked_ref[k, 0, comp, 0].astype(F32)
            lim = locked_ref[k, 1, comp, 0].astype(F32)
            re = re - one[k] * lre + two[k] * lim
            im = im - one[k] * lim - two[k] * lre
        real.append(re)
        imag.append(im)

    def cross(v):
        return [qy * v[2] - qz * v[1], qz * v[0] - qx * v[2], qx * v[1] - qy * v[0]]

    curl_re = [-v for v in cross(imag)]
    curl_im = cross(real)
    lines = right_dft(jnp.concatenate(curl_re, axis=0), tz_ref[0, :grid_len], tz_ref[1, :grid_len])
    lines += right_dft(jnp.concatenate(curl_im, axis=0), tz_ref[0, grid_len:], tz_ref[1, grid_len:])
    for comp in range(3):
        part = lines[comp * grid_len:(comp + 1) * grid_len]
        out = left_dft(ty_ref, [part[:, t * 128:(t + 1) * 128] for t in range(3)])
        for j in range(ly):
            for t in range(3):
                at = t * rows + step * (3 * ly) + comp * ly + j
                out_ref[pl.ds(at, n, stride=3 * rows), :] = out[j * n:(j + 1) * n, t * 128:(t + 1) * 128]


def mid_kernel(sizes, x_ref, diag_ref, corr_ref, ti_ref, tf_ref, out_ref, acc_ref):
    n, rows, lx, ly, kept, grid_len = sizes
    step = pl.program_id(0)

    @pl.when(step == 0)
    def _():
        acc_ref[...] = jnp.zeros_like(acc_ref)

    space = []
    for comp in range(3):
        tiles = []
        for t in range(3):
            at = [t * rows + x * (3 * ly) + comp * ly + step for x in range(lx)]
            tiles.append(
                jnp.concatenate([x_ref[pl.ds(a, n, stride=3 * rows), :] for a in at], axis=0)
            )
        out = left_dft(ti_ref, tiles)
        space.append([out[:, t * 128:(t + 1) * 128] for t in range(3)])

    def lanes(e):
        tail = e[:, 128:]
        return [e[:, :128], jnp.concatenate([tail, tail], axis=1)]

    dx, dy, dz = diag_ref[0, 0], diag_ref[1, 0], diag_ref[2, 0]
    exy = lanes(corr_ref[0, 0] * jnp.sqrt(dx * dy))
    exz = lanes(corr_ref[1, 0] * jnp.sqrt(dx * dz))
    eyz = lanes(corr_ref[2, 0] * jnp.sqrt(dy * dz))
    exx, eyy, ezz = lanes(dx), lanes(dy), lanes(dz)
    matrix = [[exx, exy, exz], [exy, eyy, eyz], [exz, eyz, ezz]]
    sum_re = jnp.zeros((grid_len, 128), F32)
    sum_im = jnp.zeros((grid_len, 128), F32)
    for comp in range(3):
        tiles = []
        for t in range(3):
            e = [matrix[comp][b][t % 2] for b in range(3)]
            tiles.append(e[0] * space[0][t] + e[1] * space[1][t] + e[2] * space[2][t])
        turned = times_i(tiles)
        for t in range(3):
            sum_re += space[comp][t] * tiles[t]
            sum_im -= space[comp][t] * turned[t]
        out = left_dft(tf_ref, tiles)
        for x in range(lx):
            for t in range(3):
                at = t * rows + x * (3 * ly) + comp * ly + step
                out_ref[pl.ds(at, n, stride=3 * rows), :] = out[x * n:(x + 1) * n, t * 128:(t + 1) * 128]
    acc_ref[0:1] += jnp.sum(sum_re, axis=0, keepdims=True)
    acc_ref[1:2] += jnp.sum(sum_im, axis=0, keepdims=True)

    @pl.when(step == pl.num_programs(0) - 1)
    def _():
        for t in range(3):
            for r in range(3 * lx * ly, rows):
                value = jnp.broadcast_to(acc_ref[min(t, 1):min(t, 1) + 1], (n, 128))
                out_ref[pl.ds(t * rows + r, n, stride=3 * rows), :] = value


def home_kernel(sizes, wave_ref, x_ref, qy_ref, qz_ref, ty_ref, tz_ref, out_ref, ray_ref):
    n, rows, lx, ly, kept, grid_len = sizes
    step = pl.program_id(0)
    qx = wave_ref[step]
    qy = qy_ref[...]
    qz = qz_ref[...]
    lines = []
    for comp in range(3):
        tiles = []
        for t in range(3):
            at = [t * rows + step * (3 * ly) + comp * ly + j for j in range(ly)]
            tiles.append(
                jnp.concatenate([x_ref[pl.ds(a, n, stride=3 * rows), :] for a in at], axis=0)
            )
        lines.append(left_dft(ty_ref, tiles))
    lines = jnp.concatenate(lines, axis=0)
    both = [right_dft(lines, tz_ref[2 * p], tz_ref[2 * p + 1]) for p in range(2)]
    real, imag = [[b[c * grid_len:(c + 1) * grid_len] for c in range(3)] for b in both]

    def cross(v):
        return [qy * v[2] - qz * v[1], qz * v[0] - qx * v[2], qx * v[1] - qy * v[0]]

    for comp, (a, b) in enumerate(zip(cross(imag), cross(real))):
        out_ref[0, 0, comp, 0] = (-a).astype(BF16)
        out_ref[0, 1, comp, 0] = b.astype(BF16)

    @pl.when(step == pl.num_programs(0) - 1)
    def _():
        for p in range(2):
            ray_ref[p * n:(p + 1) * n, :] = x_ref[pl.ds(p * rows + 3 * lx * ly, n, stride=3 * rows), :]


def exchange(flat, n):
    box = flat.reshape(n, flat.shape[0] // n, flat.shape[1])
    return lax.all_to_all(box, "wide", 0, 0, tiled=True).reshape(flat.shape)


def per_device(trial_bands, locked_bands, inv_diag, inv_corr):
    kept = locked_bands.shape[0]
    lx = trial_bands.shape[3]
    grid_len = trial_bands.shape[4]
    n = grid_len // lx
    ly = inv_diag.shape[2]
    rows = (3 * lx * ly + 8) // 8 * 8
    sizes = (n, rows, lx, ly, kept, grid_len)
    me = lax.axis_index("wide")
    fields = 2 * kept + 2

    def params():
        return pltpu.CompilerParams(vmem_limit_bytes=VMEM_LIMIT, dimension_semantics=("arbitrary",))

    def full(a):
        return pl.BlockSpec(a.shape, lambda i: (0,) * a.ndim)

    plane = lambda lead: pl.BlockSpec(
        (lead, 2, 3, 1, grid_len, grid_len), lambda i: (0, 0, 0, i, 0, 0)
    )
    smem = pl.BlockSpec(memory_space=pltpu.SMEM)

    part = pl.pallas_call(
        functools.partial(gram_kernel, kept),
        grid=(lx,),
        out_shape=jax.ShapeDtypeStruct((16, 128), F32),
        in_specs=[plane(kept), plane(1)],
        out_specs=pl.BlockSpec((16, 128), lambda i: (0, 0)),
        scratch_shapes=[pltpu.VMEM((fields * 16, fields * 16), F32)],
        compiler_params=params(),
    )(locked_bands, trial_bands)
    sums = sum_small(part, n)
    k2 = 2 * kept
    rr, ri = sums[:kept, :kept], sums[:kept, kept:k2]
    ir, ii = sums[kept:k2, :kept], sums[kept:k2, kept:k2]
    gram_a, gram_q = rr + ii, ir - ri
    proj_re = sums[:kept, k2:k2 + 1] + sums[kept:k2, k2 + 1:k2 + 2]
    proj_im = sums[:kept, k2 + 1:k2 + 2] - sums[kept:k2, k2:k2 + 1]
    gram = jnp.concatenate(
        [jnp.concatenate([gram_a, gram_q], axis=1), jnp.concatenate([gram_q.T, gram_a], axis=1)],
        axis=0,
    )
    rhs = jnp.concatenate([proj_re, proj_im], axis=0)
    lower = jnp.linalg.cholesky(gram)
    middle = lax.linalg.triangular_solve(lower, rhs, left_side=True, lower=True)
    coef = lax.linalg.triangular_solve(lower, middle, left_side=True, lower=True, transpose_a=True)
    coef = coef[:, 0]

    waves = signed(grid_len)
    wave_x = lax.dynamic_slice(jnp.asarray(waves), (me * lx,), (lx,))
    qy = jnp.asarray(np.broadcast_to(waves[:, None], (grid_len, grid_len)))
    qz = jnp.asarray(np.broadcast_to(waves[None, :], (grid_len, grid_len)))
    order_y = np.arange(grid_len).reshape(n, ly).T.reshape(-1)
    order_x = np.arange(grid_len).reshape(n, lx).T.reshape(-1)
    tz_out = jnp.asarray(split_np(right_table(grid_len, 1.0)))
    ty_out = jnp.asarray(np.concatenate(split_np(left_table(grid_len, 1.0, perm_rows=order_y))))
    tx_in = jnp.asarray(np.concatenate(split_np(left_table(grid_len, 1.0, perm_cols=order_x))))
    tx_out = jnp.asarray(np.concatenate(split_np(left_table(grid_len, -1.0, perm_rows=order_x))))
    ty_in = jnp.asarray(np.concatenate(split_np(left_table(grid_len, -1.0, perm_cols=order_y))))
    back = right_table_back(grid_len, -1.0)
    tz_in = jnp.asarray(
        np.concatenate([split_np(back[:, :grid_len]), split_np(back[:, grid_len:])])
    )

    flat_shape = jax.ShapeDtypeStruct((n * 3 * rows, 128), F32)
    flat_spec = pl.BlockSpec((n * 3 * rows, 128), lambda i: (0, 0))
    moved = pl.pallas_call(
        functools.partial(out_kernel, sizes),
        grid=(lx,),
        out_shape=flat_shape,
        in_specs=[smem, smem, plane(kept), plane(1), full(qy), full(qz), full(tz_out), full(ty_out)],
        out_specs=flat_spec,
        compiler_params=params(),
    )(coef, wave_x, locked_bands, trial_bands, qy, qz, tz_out, ty_out)
    moved = exchange(moved, n)

    slab = pl.BlockSpec((3, 1, grid_len, grid_len), lambda i: (0, i, 0, 0))
    weighted = pl.pallas_call(
        functools.partial(mid_kernel, sizes),
        grid=(ly,),
        out_shape=flat_shape,
        in_specs=[flat_spec, slab, slab, full(tx_in), full(tx_out)],
        out_specs=flat_spec,
        scratch_shapes=[pltpu.VMEM((8, 128), F32)],
        compiler_params=params(),
    )(moved, inv_diag.transpose(0, 2, 1, 3), inv_corr.transpose(0, 2, 1, 3), tx_in, tx_out)
    home = exchange(weighted, n)

    applied, ray = pl.pallas_call(
        functools.partial(home_kernel, sizes),
        grid=(lx,),
        out_shape=(
            jax.ShapeDtypeStruct(trial_bands.shape, BF16),
            jax.ShapeDtypeStruct((2 * n, 128), F32),
        ),
        in_specs=[smem, flat_spec, full(qy), full(qz), full(ty_in), full(tz_in)],
        out_specs=(plane(1), pl.BlockSpec((2 * n, 128), lambda i: (0, 0))),
        compiler_params=params(),
    )(wave_x, home, qy, qz, ty_in, tz_in)
    scale_all = 1.0 / float(grid_len * grid_len * grid_len)
    rayleigh = jnp.sum(ray.reshape(2, n * 128), axis=1).reshape(2, 1, 1) * scale_all
    return (applied, rayleigh)


def solution(mesh):
    in_specs = (
        P("groups", None, None, "wide", None, None),
        P("groups", None, None, "wide", None, None),
        P("groups", None, "wide", None),
        P("groups", None, "wide", None),
    )
    out_specs = (P("groups", None, None, "wide", None, None), P("groups", None, None))
    return jax.shard_map(
        per_device, mesh=mesh, in_specs=in_specs, out_specs=out_specs, check_vma=False
    )
```
